32 devices in a mesh: grp: 2 (over y), tp: 4 (over z), pp: 2 (over x), rep: 2 (over core).
Axes of the slice: x: 2, y: 2, z: 4, core: 2. Of those that a mesh axis runs over, the one named last changes fastest.
Arguments:
- first_tokens: bfloat16 [32, 14336], P('grp', 'tp'), parts along dimension 0, may hold values from -6 to 6
- second_tokens: bfloat16 [32, 14336], P('grp', 'tp'), parts along dimension 0, may hold values from -6 to 6
- qkv_weight: bfloat16 [14336, 3, 64, 128], P('tp', None, ('pp', 'rep')), may hold values from -0.046875 to 0.046875
- cache: bfloat16 [32, 64, 2, 64, 128], P(('grp', 'tp'), None, None, ('pp', 'rep')), parts along dimension 0, may hold values from -6 to 6
- lengths: int32 [32], P('grp'), parts along dimension 0, may hold values from 1 to 62, 496 in all
- matching: int32 [8], P('grp'), parts along dimension 0, may hold values from 0 to 3, as said below
Outputs:
- attended: bfloat16 [2, 32, 8192], P(None, ('grp', 'tp'), ('pp', 'rep')), parts along dimension 1
- new_cache: bfloat16 [32, 64, 2, 64, 128], P(('grp', 'tp'), None, None, ('pp', 'rep')), parts along dimension 0
The draws below stay inside these ranges and needn't reach their ends.
There are 2 independent parts, one for each index of `grp`. The reference program is written for one: setup_inputs(seed, part) draws one part's arguments, and reference() takes and returns one part's arrays. A program takes and returns all parts, laid end to end along the dimension named above; an argument that names none is the same for every part. Nothing has to cross between parts.
Inputs may be any that keep to these rules, and one draw needn't show every extreme that they name: matching[t] = (t + matching[0]) mod 4 for every t: all old owners move by one common offset.
All inputs are finite; a program needn't handle non-finite values.
Results may differ from the reference program's by a relative error of at most 0.012.
Values may be sent and summed in bfloat16 or wider, within the bound.
No kernel may reach another device: no remote copies, remote signals or barrier semaphores. Data moves between devices by JAX's collectives and lax.ppermute only.
A program may use at most 128 MiB of HBM per device.

```python
import math
import jax
import jax.numpy as jnp
import numpy as np

D = 14336
HD = 128
HEADS = 64
REQ_DEV = 4
L = 64
B = 16
OWNERS = 4


def draw_matching(key, part):
    key = jax.random.fold_in(key, 7)
    offset = jax.random.randint(key, (), 0, OWNERS, dtype=jnp.int32)
    return ((jnp.arange(OWNERS, dtype=jnp.int32) + offset) % OWNERS).astype(jnp.int32)


def block_scale(stream_key, dims, split, low, largest):
    gain, own = 1.0, jax.random.fold_in(stream_key, 6)
    for axis_at, blocks in split:
        steps = jnp.exp(jax.random.uniform(jax.random.fold_in(own, axis_at), (blocks,), jnp.float32, low / len(split), largest / len(split)))
        gain = gain * jnp.repeat(steps, dims[axis_at] // blocks).reshape([-1 if axis == axis_at else 1 for axis in range(len(dims))])
    return gain


def profile(number_of, total, bound, lean):
    weights = [(1 << 20) // math.isqrt(grade ** lean) + 1 for grade in range(2, number_of + 1)]
    spare, counts = total - bound - (number_of - 1), [1] * (number_of - 1)
    while spare > 0:
        movable = [i for i in range(number_of - 1) if counts[i] < bound]
        whole, remaining = sum([weights[i] for i in movable]), spare
        for i in movable:
            addition = min(bound - counts[i], max(1, remaining * weights[i] // whole), spare)
            counts[i] = counts[i] + addition
            spare = spare - addition
    return np.array([bound] + counts)


def ragged(own_key, number_of, total, reach, slope):
    if number_of == 2:
        one = jax.random.randint(own_key, (), max(1, total - reach), min(reach, total - 1) + 1)
        return jnp.stack([one, total - one])
    sizes = jnp.asarray(profile(number_of, total, reach, slope), jnp.int32)
    twos = (number_of - 1) // 2
    source_of, receiver = sizes[1:1 + 2 * twos:2], sizes[2:2 + 2 * twos:2]
    room = jnp.minimum(source_of - 1, reach - receiver)
    moved = jax.random.randint(jax.random.fold_in(own_key, 1), (twos,), 0, 1 << 20) % (room + 1)
    sizes = sizes.at[1:1 + 2 * twos:2].set(source_of - moved).at[2:2 + 2 * twos:2].set(receiver + moved)
    return sizes[jax.random.permutation(jax.random.fold_in(own_key, 2), number_of)]


def noise(rng, extent, width, reach, cuts=(), held_as=jnp.bfloat16):
    level = block_scale(rng, extent, cuts, -0.22, 0.18) if cuts else 1.0
    drawn = jax.random.normal(rng, extent, jnp.float32) * width * level
    return jnp.minimum(jnp.maximum(drawn, -reach), reach).astype(held_as)


def setup_inputs(seed: int = 0, part: int = 0) -> dict:
    streams_of = jax.random.split(jax.random.key(seed), 7)
    part_splits = jax.random.split(jax.random.fold_in(streams_of[6], part), 7)
    first_tokens = noise(part_splits[0], (B, D), 1.0, 6.0, ((1, 4),))
    second_tokens = noise(part_splits[1], (B, D), 1.0, 6.0, ((1, 4),))
    qkv_weight = noise(streams_of[2], (D, 3, HEADS, HD), D ** -0.5, 0.046875, ((0, 4), (2, 4)))
    cache = noise(part_splits[3], (B, L, 2, HEADS, HD), 1.0, 6.0, ((0, 4), (3, 4)))
    lengths = ragged(part_splits[4], B, B * (L - 2) // 2, L - 2, 2).astype(jnp.int32)
    matching = draw_matching(jax.random.fold_in(jax.random.fold_in(streams_of[6], part), 71), part)
    return dict(first_tokens=first_tokens, second_tokens=second_tokens, qkv_weight=qkv_weight, cache=cache, lengths=lengths, matching=matching)


def project(tokens, qkv_weight):
    flat_weight = qkv_weight.reshape(D, 3 * HEADS * HD)
    summed = jnp.dot(tokens, flat_weight, preferred_element_type=jnp.float32)
    return summed.astype(jnp.bfloat16).reshape(B, 3, HEADS, HD)


def attend(query, filled, position):
    keys_all = filled[:, :, 0].astype(jnp.float32)
    values_all = filled[:, :, 1].astype(jnp.float32)
    scores = jnp.einsum("bhd,blhd->bhl", query.astype(jnp.float32), keys_all) * (HD ** -0.5)
    slopes = 2.0 ** (-(jnp.arange(HEADS, dtype=jnp.int32) + 1.0) / 8.0)
    spots = jnp.arange(L, dtype=jnp.int32)
    distance = (position[:, None] - spots[None, :]).astype(jnp.float32)
    scores = scores - slopes[None, :, None] * distance[:, None, :]
    valid = spots[None, :] <= position[:, None]
    scores = jnp.where(valid[:, None, :], scores, -1e30)
    weights = jax.nn.softmax(scores, axis=-1).astype(jnp.bfloat16)
    mixed = jnp.einsum("bhl,blhd->bhd", weights.astype(jnp.float32), values_all)
    return mixed.astype(jnp.bfloat16).reshape(B, HEADS * HD)


def reference(first_tokens, second_tokens, qkv_weight, cache, lengths, matching):
    requests = jnp.arange(B, dtype=jnp.int32)
    target = (matching[requests // REQ_DEV] * REQ_DEV + requests % REQ_DEV).astype(jnp.int32)
    moved = jnp.zeros_like(cache).at[target].set(cache)
    position = jnp.zeros_like(lengths).at[target].set(lengths)
    projected = [project(first_tokens, qkv_weight), project(second_tokens, qkv_weight)]
    spots = jnp.arange(L, dtype=jnp.int32)
    for step_index in range(2):
        fresh = projected[step_index][:, 1:]
        hit = spots[None, :] == (position + step_index)[:, None]
        moved = jnp.where(hit[:, :, None, None, None], fresh[:, None], moved)
    attended = jnp.stack([attend(projected[step_index][:, 0], moved, position + step_index) for step_index in range(2)])
    return attended, moved
```

```python
import math

import jax
import jax.numpy as jnp
from jax import lax
from jax.experimental import pallas as pl
from jax.experimental.pallas import tpu as pltpu
from jax.sharding import PartitionSpec as P

WIDEST_SWITCH = 8


def shifted(block, axis, by):
    devices = lax.axis_size(axis)
    return lax.ppermute(block, axis, [(i, (i + by) % devices) for i in range(devices)])


def rotate_by_bits(block, offset, owners):
    for level in range((owners - 1).bit_length()):
        moved = shifted(block, "tp", 1 << level)
        block = jnp.where(offset >> level & 1 == 1, moved, block)
    return block


def owner_order(owners):
    order = [0]
    for level in reversed(range((owners - 1).bit_length())):
        order = order + [i ^ (1 << level) for i in order]
    return order


def reduce_to_owner(parts, owners):
    order = owner_order(owners)
    for level in range((owners - 1).bit_length()):
        half = parts.shape[0] // 2
        kept, sent = parts[:half], parts[half:].astype(jnp.bfloat16)
        assert all(order[half + j] == order[j] ^ (1 << level) for j in range(half))
        got = lax.ppermute(sent, "tp", [(i, i ^ (1 << level)) for i in range(owners)])
        parts = kept + got.astype(jnp.float32)
        order = order[:half]
    return parts[0]


def attention_kernel(
    lengths_ref, matching_ref, fresh_ref, cache_ref, moved_ref, attended_ref, filled_ref, block, mixed, result, in_sems, out_sems, result_sem
):
    rows, spots, _, heads, head_dim = block.shape
    steps = fresh_ref.shape[0]
    stays = matching_ref[0] == 0
    loads = [pltpu.make_async_copy(moved_ref.at[r], block.at[r], in_sems.at[r]) for r in range(rows)]
    for r in range(rows):

        @pl.when(stays)
        def _(r=r):
            pltpu.make_async_copy(cache_ref.at[r], block.at[r], in_sems.at[r]).start()

        @pl.when(jnp.logical_not(stays))
        def _(r=r):
            loads[r].start()

    owners = lax.axis_size("tp")
    first_row = lax.rem(lax.axis_index("tp") - matching_ref[0] + owners, owners) * rows
    first_head = lax.axis_index(("pp", "rep")) * heads
    head = (first_head + 1 + lax.broadcasted_iota(jnp.int32, (heads, 1), 0)).astype(jnp.float32)
    slopes = jnp.exp(head * (-math.log(2.0) / 8.0))
    spot = lax.broadcasted_iota(jnp.int32, (spots, heads, 1), 0)
    stores = []
    for r in range(rows):
        loads[r].wait()
        at = lengths_ref[first_row + r]
        for s in range(steps):
            for part in range(2):
                block[r, at + s, part] = fresh_ref[s, r, 1 + part]
        stores.append(pltpu.make_async_copy(block.at[r], filled_ref.at[r], out_sems.at[r]))
        stores[-1].start()
        keys = block[r, :, 0].astype(jnp.float32)
        values = block[r, :, 1].astype(jnp.float32)
        for s in range(steps):
            query = fresh_ref[s, r, 0].astype(jnp.float32)
            scores = jnp.sum(keys * query[None], axis=-1, keepdims=True) * head_dim ** (-0.5)
            distance = (at + s) - spot
            scores = scores - slopes[None] * distance.astype(jnp.float32)
            scores = jnp.where(distance >= 0, scores, -1e30)
            weights = jnp.exp(scores - jnp.max(scores, axis=0, keepdims=True))
            total = jnp.sum(weights, axis=0)
            mixed[s, r] = jnp.sum(weights * values, axis=0) / total
    for s in range(steps):
        for h in range(heads):
            result[s, :, h * head_dim : (h + 1) * head_dim] = mixed[s, :, h].astype(result.dtype)
    finish = pltpu.make_async_copy(result, attended_ref, result_sem)
    finish.start()
    for store in stores:
        store.wait()
    finish.wait()


def unwritten(like):
    return pl.pallas_call(
        lambda out_ref: None,
        out_shape=jax.ShapeDtypeStruct(like.shape, like.dtype),
        out_specs=pl.BlockSpec(memory_space=pl.ANY),
        name="unwritten",
    )()


def attend_and_write(cache, moved, fresh, lengths, matching):
    rows, _, _, heads, head_dim = moved.shape
    steps = fresh.shape[0]
    smem = pl.BlockSpec(memory_space=pltpu.SMEM)
    anywhere = pl.BlockSpec(memory_space=pl.ANY)
    attended = jax.ShapeDtypeStruct((steps, rows, heads * head_dim), jnp.bfloat16)
    return pl.pallas_call(
        attention_kernel,
        out_shape=(attended, jax.ShapeDtypeStruct(moved.shape, moved.dtype)),
        in_specs=[smem, smem, pl.BlockSpec(memory_space=pltpu.VMEM), anywhere, anywhere],
        out_specs=(anywhere, anywhere),
        scratch_shapes=[
            pltpu.VMEM(moved.shape, moved.dtype),
            pltpu.VMEM((steps, rows, heads, head_dim), jnp.float32),
            pltpu.VMEM(attended.shape, attended.dtype),
            pltpu.SemaphoreType.DMA((rows,)),
            pltpu.SemaphoreType.DMA((rows,)),
            pltpu.SemaphoreType.DMA,
        ],
        compiler_params=pltpu.CompilerParams(vmem_limit_bytes=32 << 20),
        cost_estimate=pl.CostEstimate(flops=0, bytes_accessed=4 * moved.size, transcendentals=0),
        name="attend",
    )(lengths, matching, fresh, cache, moved)


def project(tokens, flat_weight, owners, local_rows):
    steps = tokens.shape[0]
    rank = lax.axis_index("tp")
    blocks = tokens.reshape(steps, owners, local_rows, -1)
    ordered = jnp.concatenate(
        [
            lax.dynamic_slice_in_dim(blocks, rank ^ distance, 1, 1).reshape(steps * local_rows, -1)
            for distance in owner_order(owners)
        ]
    )
    parts = jnp.dot(ordered, flat_weight, preferred_element_type=jnp.float32)
    total = reduce_to_owner(parts.reshape(owners, steps * local_rows, -1), owners)
    return total.astype(jnp.bfloat16).reshape(steps, local_rows, -1)


def shards(first_tokens, second_tokens, qkv_weight, cache, lengths, matching):
    owners = lax.axis_size("tp")
    assert owners & (owners - 1) == 0
    local_rows = cache.shape[0]
    heads_local = qkv_weight.shape[2]
    head_dim = qkv_weight.shape[3]
    offset = matching[0]

    def serve(move, first_tokens, second_tokens, qkv_weight, cache):
        projected = project(
            jnp.stack([first_tokens, second_tokens]),
            qkv_weight.reshape(qkv_weight.shape[0], -1),
            owners,
            local_rows,
        )
        return move(cache), projected

    args = (first_tokens, second_tokens, qkv_weight, cache)
    if owners > WIDEST_SWITCH:
        moved, projected = serve(lambda block: rotate_by_bits(block, offset, owners), *args)
    else:
        branches = [
            lambda *args, by=by: serve(lambda block: shifted(block, "tp", by) if by else unwritten(block), *args)
            for by in range(owners)
        ]
        moved, projected = lax.switch(offset, branches, *args)
    fresh = projected.reshape(2, local_rows, 3, heads_local, head_dim)
    return attend_and_write(cache, moved, fresh, lengths, matching)


def solution(mesh):
    in_specs = (
        P("grp", "tp"),
        P("grp", "tp"),
        P("tp", None, ("pp", "rep"), None),
        P(("grp", "tp"), None, None, ("pp", "rep"), None),
        P("grp"),
        P("grp"),
    )
    out_specs = (
        P(None, ("grp", "tp"), ("pp", "rep")),
        P(("grp", "tp"), None, None, ("pp", "rep"), None),
    )
    return jax.shard_map(shards, mesh=mesh, in_specs=in_specs, out_specs=out_specs, check_vma=False)
```

```python
import functools
import math

import jax
import jax.numpy as jnp
from jax import lax
from jax.experimental import pallas as pl
from jax.experimental.pallas import tpu as pltpu
from jax.sharding import PartitionSpec as P

WIDEST_SWITCH = 8


def shifted(block, axis, by):
    devices = lax.axis_size(axis)
    return lax.ppermute(block, axis, [(i, (i + by) % devices) for i in range(devices)])


def rotate_by_bits(block, offset, owners):
    for level in range((owners - 1).bit_length()):
        moved = shifted(block, "tp", 1 << level)
        block = jnp.where(offset >> level & 1 == 1, moved, block)
    return block


def owner_order(owners):
    order = [0]
    for level in reversed(range((owners - 1).bit_length())):
        order = order + [i ^ (1 << level) for i in order]
    return order


def reduce_by_halves(parts, owners):
    order = owner_order(owners)
    for level in range((owners - 1).bit_length()):
        half = parts.shape[0] // 2
        kept, sent = parts[:half], parts[half:].astype(jnp.bfloat16)
        assert all(order[half + j] == order[j] ^ (1 << level) for j in range(half))
        got = lax.ppermute(sent, "tp", [(i, i ^ (1 << level)) for i in range(owners)])
        parts = kept + got.astype(jnp.float32)
        order = order[:half]
    return parts[0]


def reduce_at_once(parts, owners):
    total = parts[0]
    for distance in range(1, owners):
        block = parts[owner_order(owners).index(distance)].astype(jnp.bfloat16)
        got = lax.ppermute(block, "tp", [(i, i ^ distance) for i in range(owners)])
        total = total + got.astype(jnp.float32)
    return total


def attention_kernel(
    lengths_ref, matching_ref, fresh_ref, cache_ref, moved_ref, attended_ref, filled_ref, block, mixed, result, in_sems, out_sems, result_sem
):
    rows, spots, _, heads, head_dim = block.shape
    steps = fresh_ref.shape[0]
    stays = matching_ref[0] == 0
    loads = [pltpu.make_async_copy(moved_ref.at[r], block.at[r], in_sems.at[r]) for r in range(rows)]
    for r in range(rows):

        @pl.when(stays)
        def _(r=r):
            pltpu.make_async_copy(cache_ref.at[r], block.at[r], in_sems.at[r]).start()

        @pl.when(jnp.logical_not(stays))
        def _(r=r):
            loads[r].start()

    owners = lax.axis_size("tp")
    first_row = lax.rem(lax.axis_index("tp") - matching_ref[0] + owners, owners) * rows
    first_head = lax.axis_index(("pp", "rep")) * heads
    shape = (spots * heads, steps * heads)
    row, column = (lax.broadcasted_iota(jnp.int32, shape, axis) for axis in range(2))
    spot, step = row // heads, column // heads
    own = row % heads == column % heads
    head = (first_head + 1 + column % heads).astype(jnp.float32)
    slopes = jnp.exp(head * (-math.log(2.0) / 8.0))
    since = (step - spot).astype(jnp.float32)
    allowed = jnp.where(own, step - spot, -2 * spots)
    stores = []
    for r in range(rows):
        loads[r].wait()
        at = lengths_ref[first_row + r]
        for s in range(steps):
            for part in range(2):
                block[r, at + s, part] = fresh_ref[s, r, 1 + part]
        stores.append(pltpu.make_async_copy(block.at[r], filled_ref.at[r], out_sems.at[r]))
        stores[-1].start()
        keys = block[r, :, 0].reshape(spots * heads, head_dim)
        values = block[r, :, 1].reshape(spots * heads, head_dim)
        query = fresh_ref[:, r, 0].reshape(steps * heads, head_dim)
        scores = lax.dot_general(keys, query, (((1,), (1,)), ((), ())), preferred_element_type=jnp.float32)
        scores = scores * head_dim ** (-0.5) - slopes * (since + at.astype(jnp.float32))
        scores = jnp.where(allowed + at >= 0, scores, -1e30)
        weights = jnp.exp(scores - jnp.max(scores, axis=0, keepdims=True)).astype(values.dtype)
        sums = lax.dot_general(
            weights, jnp.ones_like(values), (((0,), (0,)), ((), ())), preferred_element_type=jnp.float32
        )
        mix = lax.dot_general(weights, values, (((0,), (0,)), ((), ())), preferred_element_type=jnp.float32)
        mixed[:, r] = (mix / sums).reshape(steps, heads, head_dim)
    for s in range(steps):
        for h in range(heads):
            result[s, :, h * head_dim : (h + 1) * head_dim] = mixed[s, :, h].astype(result.dtype)
    finish = pltpu.make_async_copy(result, attended_ref, result_sem)
    finish.start()
    for store in stores:
        store.wait()
    finish.wait()


def unwritten(like):
    return pl.pallas_call(
        lambda out_ref: None,
        out_shape=jax.ShapeDtypeStruct(like.shape, like.dtype),
        out_specs=pl.BlockSpec(memory_space=pl.ANY),
        name="unwritten",
    )()


def attend_and_write(cache, moved, fresh, lengths, matching):
    rows, _, _, heads, head_dim = cache.shape
    steps = fresh.shape[0]
    smem = pl.BlockSpec(memory_space=pltpu.SMEM)
    anywhere = pl.BlockSpec(memory_space=pl.ANY)
    attended = jax.ShapeDtypeStruct((steps, rows, heads * head_dim), jnp.bfloat16)
    return pl.pallas_call(
        attention_kernel,
        out_shape=(attended, jax.ShapeDtypeStruct(cache.shape, cache.dtype)),
        in_specs=[smem, smem, pl.BlockSpec(memory_space=pltpu.VMEM), anywhere, anywhere],
        out_specs=(anywhere, anywhere),
        scratch_shapes=[
            pltpu.VMEM(cache.shape, cache.dtype),
            pltpu.VMEM((steps, rows, heads, head_dim), jnp.float32),
            pltpu.VMEM(attended.shape, attended.dtype),
            pltpu.SemaphoreType.DMA((rows,)),
            pltpu.SemaphoreType.DMA((rows,)),
            pltpu.SemaphoreType.DMA,
        ],
        compiler_params=pltpu.CompilerParams(vmem_limit_bytes=32 << 20),
        cost_estimate=pl.CostEstimate(flops=0, bytes_accessed=4 * cache.size, transcendentals=0),
        name="attend",
    )(lengths, matching, fresh, cache, moved)


def order_tokens(token_arrays, owners, local_rows):
    rank = lax.axis_index("tp")
    blocks = [tokens.reshape(owners, local_rows, -1) for tokens in token_arrays]
    return jnp.concatenate(
        [
            lax.dynamic_index_in_dim(block, rank ^ distance, 0, keepdims=False)
            for distance in owner_order(owners)
            for block in blocks
        ]
    )


def shards(first_tokens, second_tokens, qkv_weight, cache, lengths, matching):
    owners = lax.axis_size("tp")
    assert owners & (owners - 1) == 0
    local_rows = cache.shape[0]
    heads_local = qkv_weight.shape[2]
    head_dim = qkv_weight.shape[3]
    offset = matching[0]

    def serve(move, reduce, first_tokens, second_tokens, qkv_weight, cache):
        moved = move(cache)
        tokens = order_tokens((first_tokens, second_tokens), owners, local_rows)
        parts = jnp.dot(tokens, qkv_weight.reshape(qkv_weight.shape[0], -1), preferred_element_type=jnp.float32)
        total = reduce(parts.reshape(owners, 2 * local_rows, -1), owners)
        fresh = total.astype(jnp.bfloat16).reshape(2, local_rows, 3, heads_local, head_dim)
        return moved, fresh

    args = (first_tokens, second_tokens, qkv_weight, cache)
    if owners > WIDEST_SWITCH:
        moved = serve(lambda block: rotate_by_bits(block, offset, owners), reduce_by_halves, *args)
    else:
        branches = []
        for by in range(owners):
            hops = min(by, owners - by)
            move = functools.partial(shifted, axis="tp", by=by) if by else unwritten
            branches.append(functools.partial(serve, move, reduce_by_halves if hops > 1 else reduce_at_once))
        moved = lax.switch(offset, branches, *args)
    return attend_and_write(cache, *moved, lengths, matching)


def solution(mesh):
    in_specs = (
        P("grp", "tp"),
        P("grp", "tp"),
        P("tp", None, ("pp", "rep"), None),
        P(("grp", "tp"), None, None, ("pp", "rep"), None),
        P("grp"),
        P("grp"),
    )
    out_specs = (
        P(None, ("grp", "tp"), ("pp", "rep")),
        P(("grp", "tp"), None, None, ("pp", "rep"), None),
    )
    return jax.shard_map(shards, mesh=mesh, in_specs=in_specs, out_specs=out_specs, check_vma=False)
```

```python
import functools
import math

import jax
import jax.numpy as jnp
from jax import lax
from jax.experimental import pallas as pl
from jax.experimental.pallas import tpu as pltpu
from jax.sharding import PartitionSpec as P

WIDEST_SWITCH = 8


def shifted(block, axis, by):
    devices = lax.axis_size(axis)
    return lax.ppermute(block, axis, [(i, (i + by) % devices) for i in range(devices)])


def rotate_by_bits(block, offset, owners):
    for level in range((owners - 1).bit_length()):
        moved = shifted(block, "tp", 1 << level)
        block = jnp.where(offset >> level & 1 == 1, moved, block)
    return block


def reduce_by_halves(parts, owners):
    distances = list(range(owners))
    blocks = [parts[distance] for distance in distances]
    stride = 1
    while stride < owners:
        kept = [i for i, distance in enumerate(distances) if not distance & stride]
        gone = [i for i, distance in enumerate(distances) if distance & stride]
        sent = jnp.stack([blocks[i] for i in gone]).astype(jnp.bfloat16)
        got = lax.ppermute(sent, "tp", [(i, i ^ stride) for i in range(owners)]).astype(jnp.float32)
        blocks = [blocks[i] + got[j] for j, i in enumerate(kept)]
        distances = [distances[i] for i in kept]
        stride *= 2
    return blocks[0]


def reduce_at_once(parts, owners):
    total = parts[0]
    for distance in range(1, owners):
        pairs = [(i, i ^ distance) for i in range(owners)]
        total = total + lax.ppermute(parts[distance].astype(jnp.bfloat16), "tp", pairs).astype(jnp.float32)
    return total


UNITS = 8
LENT_TO_BUSY, LENT_TO_IDLE = 2, 3


def slot_units():
    return {
        "whole": (0, UNITS),
        "most": (0, UNITS - LENT_TO_BUSY),
        "own": (UNITS - LENT_TO_BUSY, LENT_TO_BUSY),
        "lent": (UNITS - LENT_TO_BUSY, LENT_TO_BUSY),
        "more": (0, UNITS - LENT_TO_IDLE),
        "lent_more": (UNITS - LENT_TO_IDLE, LENT_TO_IDLE),
    }


def slot_is_mine(name, mine, other):
    moves, lends, helps = mine != 0, (mine == 2) & (other != 2), (mine != 2) & (other == 2)
    return {
        "whole": moves & jnp.logical_not(lends | helps),
        "most": moves & (other != 0) & (lends | helps),
        "own": moves & helps,
        "lent": lends & (other != 0),
        "more": lends & (other == 0),
        "lent_more": lends & (other == 0),
    }[name]


def attention_kernel(names, lengths_ref, matching_ref, other_ref, fresh_ref, cache_ref, *refs):
    slots = dict(zip(names, refs))
    attended_ref, filled_ref, block, mixed, result, load_sems, row_sems, token_sems, result_sem = refs[len(names) :]
    part, _, heads, head_dim = block.shape[1:]
    steps, rows = fresh_ref.shape[:2]
    per_row = UNITS // rows
    spots = per_row * part
    owners = lax.axis_size("tp")
    mine, other = matching_ref[0], other_ref[0]
    of_row = [block.at[pl.ds(r * per_row, per_row)] for r in range(rows)]
    arrivals = [pltpu.make_async_copy(cache_ref.at[pl.ds(r * per_row, per_row)], of_row[r], load_sems.at[r]) for r in range(rows)]
    stores = [pltpu.make_async_copy(of_row[r], filled_ref.at[pl.ds(r * per_row, per_row)], row_sems.at[r]) for r in range(rows)]

    def load(source, first, count):
        unit = first
        while unit < first + count:
            size = min(first + count, (unit // per_row + 1) * per_row) - unit
            pltpu.make_async_copy(
                source.at[pl.ds(unit - first, size)], block.at[pl.ds(unit, size)], load_sems.at[unit // per_row]
            ).start()
            unit += size

    @pl.when(mine == 0)
    def _():
        load(cache_ref, 0, UNITS)

    for name in names:

        @pl.when((mine != 0) if len(names) == 1 else slot_is_mine(name, mine, other))
        def _(name=name):
            load(slots[name], *slot_units()[name])

    first_row = lax.rem(lax.axis_index("tp") - matching_ref[0] + owners, owners) * rows
    first_head = lax.axis_index(("pp", "rep")) * heads
    level = heads.bit_length() - 1
    assert heads == 1 << level

    def relation(columns):
        shape = (steps * heads, columns * heads)
        row, column = (lax.broadcasted_iota(jnp.int32, shape, axis) for axis in range(2))
        head = (first_head + 1 + (row & (heads - 1))).astype(jnp.float32)
        slope = jnp.exp(head * (-math.log(2.0) / 8.0))
        return (row >> level) - (column >> level), (row ^ column) & (heads - 1) == 0, slope

    since, own, slope = relation(spots)
    bias = slope * since.astype(jnp.float32)
    place = lax.broadcasted_iota(jnp.int32, since.shape, 1) >> level
    place = jnp.where(own, place, spots)
    since, own, fresh_slope = relation(steps)
    fresh_bias = fresh_slope * since.astype(jnp.float32)
    fresh_allowed = own & (since >= 0)

    def scored(query, keys):
        scores = lax.dot_general(query, keys, (((1,), (1,)), ((), ())), preferred_element_type=jnp.float32)
        return scores * head_dim ** (-0.5)

    def weighed(weights, values):
        paired = jnp.concatenate([values, jnp.ones_like(values)], axis=1)
        return jnp.dot(weights.astype(values.dtype), paired, preferred_element_type=jnp.float32)

    for r in range(rows):
        arrivals[r].wait()
        stores[r].start()
    for r in range(rows):
        at = lengths_ref[first_row + r]
        query, fresh_keys, fresh_values = (
            fresh_ref[:, r, kind].reshape(steps * heads, head_dim) for kind in range(3)
        )
        before = scored(query, block[r * per_row : (r + 1) * per_row, :, 0].reshape(spots * heads, head_dim))
        before = before - (bias + slope * at.astype(jnp.float32))
        before = jnp.where(place < at, before, -1e30)
        fresh = jnp.where(fresh_allowed, scored(query, fresh_keys) - fresh_bias, -1e30)
        top = jnp.maximum(jnp.max(before, axis=1, keepdims=True), jnp.max(fresh, axis=1, keepdims=True))
        mix = weighed(jnp.exp(before - top), block[r * per_row : (r + 1) * per_row, :, 1].reshape(spots * heads, head_dim))
        mix = mix + weighed(jnp.exp(fresh - top), fresh_values)
        mixed[:, r] = (mix[:, :head_dim] / mix[:, head_dim:]).reshape(steps, heads, head_dim)
    tokens = []
    for r in range(rows):
        at = lengths_ref[first_row + r]
        stores[r].wait()
        for s in range(steps):
            unit, spot = r * per_row + lax.div(at + s, part), lax.rem(at + s, part)
            token = pltpu.make_async_copy(
                fresh_ref.at[s, r, pl.ds(1, 2)], filled_ref.at[unit, spot], token_sems.at[r, s]
            )
            token.start()
            tokens.append(token)
    for s in range(steps):
        for h in range(heads):
            result[s, :, h * head_dim : (h + 1) * head_dim] = mixed[s, :, h].astype(result.dtype)
    finish = pltpu.make_async_copy(result, attended_ref, result_sem)
    finish.start()
    for token in tokens:
        token.wait()
    finish.wait()


def unwritten(shape, dtype):
    return pl.pallas_call(
        lambda out_ref: None,
        out_shape=jax.ShapeDtypeStruct(shape, dtype),
        out_specs=pl.BlockSpec(memory_space=pl.ANY),
        name="unwritten",
    )()


def attend_and_write(units, slots, fresh, lengths, matching, other):
    steps, rows, _, heads, head_dim = fresh.shape
    smem, vmem = (pl.BlockSpec(memory_space=space) for space in (pltpu.SMEM, pltpu.VMEM))
    anywhere = pl.BlockSpec(memory_space=pl.ANY)
    attended = jax.ShapeDtypeStruct((steps, rows, heads * head_dim), jnp.bfloat16)
    return pl.pallas_call(
        functools.partial(attention_kernel, tuple(slots)),
        out_shape=(attended, jax.ShapeDtypeStruct(units.shape, units.dtype)),
        in_specs=[smem, smem, smem, vmem, anywhere] + [anywhere] * len(slots),
        out_specs=(anywhere, anywhere),
        scratch_shapes=[
            pltpu.VMEM(units.shape, units.dtype),
            pltpu.VMEM((steps, rows, heads, head_dim), jnp.float32),
            pltpu.VMEM(attended.shape, attended.dtype),
            pltpu.SemaphoreType.DMA((rows,)),
            pltpu.SemaphoreType.DMA((rows,)),
            pltpu.SemaphoreType.DMA((rows, steps)),
            pltpu.SemaphoreType.DMA,
        ],
        compiler_params=pltpu.CompilerParams(vmem_limit_bytes=32 << 20),
        cost_estimate=pl.CostEstimate(flops=0, bytes_accessed=4 * units.size, transcendentals=0),
        name="attend",
    )(lengths, matching, other, fresh, units, *slots.values())


def projection_kernel(piece, first_ref, second_ref, weight_ref, parts_ref, sums):
    step = pl.program_id(0)
    kinds, pairs, _, width = sums.shape
    owners, rows = parts_ref.shape[0], parts_ref.shape[3]

    @pl.when(step == 0)
    def _():
        sums[...] = jnp.zeros_like(sums)

    count = owners * rows
    to, source = (lax.broadcasted_iota(jnp.int32, (count, count), axis) for axis in range(2))
    local_rows = rows // 2
    block, token_step, row = lax.div(to, rows), lax.div(lax.rem(to, rows), local_rows), lax.rem(to, local_rows)
    owner = block ^ lax.axis_index("tp")
    picks = (token_step * owners + owner) * local_rows + row == source
    picks = jnp.where(picks, 1.0, 0.0).astype(first_ref.dtype)
    pieces = weight_ref.shape[0] // piece

    def add(index, carry):
        kind = lax.rem(index, kinds)
        depth = pl.ds(pl.multiple_of(lax.div(index, kinds) * piece, piece), piece) if pieces > 1 else slice(None)
        tokens = jnp.concatenate([first_ref[:, depth], second_ref[:, depth]])
        tokens = jnp.dot(picks, tokens, preferred_element_type=jnp.float32).astype(tokens.dtype)
        by_head = jnp.swapaxes(weight_ref[depth, kind], 0, 1)
        for pair in range(pairs):
            both = jnp.concatenate([by_head[2 * pair], by_head[2 * pair + 1]], axis=1)
            sums[kind, pair] += jnp.dot(tokens, both, preferred_element_type=jnp.float32)
        return carry

    lax.fori_loop(0, pieces * kinds, add, 0)

    @pl.when(step == pl.num_programs(0) - 1)
    def _():
        for distance in range(owners):
            parts_ref[distance] = sums[:, :, distance * rows : (distance + 1) * rows]


def largest_divisor(number, most, unit):
    return max(size for size in range(unit, most + 1, unit) if number % size == 0)


def multiply(first_tokens, second_tokens, weight, owners):
    depth, kinds, heads, head_dim = weight.shape
    block = largest_divisor(depth, 512, 64)
    piece = 256 if block % 256 == 0 else block
    requests = first_tokens.shape[0]
    sums = (kinds, heads // 2, 2 * requests, 2 * head_dim)
    parts = (owners, kinds, heads // 2, 2 * requests // owners, 2 * head_dim)
    return pl.pallas_call(
        functools.partial(projection_kernel, piece),
        out_shape=jax.ShapeDtypeStruct(parts, jnp.float32),
        grid=(depth // block,),
        in_specs=[
            pl.BlockSpec((requests, block), lambda step: (0, step)),
            pl.BlockSpec((requests, block), lambda step: (0, step)),
            pl.BlockSpec((block, kinds, heads, head_dim), lambda step: (step, 0, 0, 0)),
        ],
        out_specs=pl.BlockSpec(parts, lambda step: (0,) * len(parts)),
        scratch_shapes=[pltpu.VMEM(sums, jnp.float32)],
        compiler_params=pltpu.CompilerParams(vmem_limit_bytes=48 << 20),
        cost_estimate=pl.CostEstimate(
            flops=4 * requests * weight.size, bytes_accessed=2 * weight.size, transcendentals=0
        ),
        name="project",
    )(first_tokens, second_tokens, weight)


def move_alone(units, by, owners):
    return {"whole": shifted(units, "tp", by)} if by else {}


def move_helped(units, heavy, by, owners):
    light = 1 - heavy

    def send(block, pairs):
        return lax.ppermute(block, ("grp", "tp"), pairs)

    def at(group, owner):
        return group * owners + owner % owners

    own = [(at(light, t), at(light, t + by)) for t in range(owners) if by]
    direct = [(at(heavy, t), at(heavy, t + 2)) for t in range(owners)] + own
    over = [(at(heavy, t), at(light, t)) for t in range(owners)]
    back = [(at(light, t), at(heavy, t + 2)) for t in range(owners)]
    split = UNITS - (LENT_TO_BUSY if by else LENT_TO_IDLE)
    most, last = units[:split], units[split:]
    lent = send(send(last, over), back)
    if by:
        return {"most": send(most, direct), "own": send(last, own), "lent": lent}
    return {"more": send(most, direct), "lent_more": lent}


def shards(first_tokens, second_tokens, qkv_weight, cache, lengths, matching):
    owners, groups = lax.axis_size("tp"), lax.axis_size("grp")
    assert owners & (owners - 1) == 0
    local_rows = cache.shape[0]
    heads_local = qkv_weight.shape[2]
    head_dim = qkv_weight.shape[3]
    units = cache.reshape(UNITS, -1, *cache.shape[2:])
    mine = matching[:1]

    def finish(fresh, slots, other):
        attended, filled = attend_and_write(units, slots, fresh, lengths, matching, other)
        return attended, filled.reshape(cache.shape)

    def project(reduce, first_tokens, second_tokens, qkv_weight):
        total = reduce(multiply(first_tokens, second_tokens, qkv_weight, owners), owners)
        fresh = total.astype(jnp.bfloat16).reshape(3, heads_local // 2, 2, local_rows, 2, head_dim)
        return fresh.transpose(2, 3, 0, 1, 4, 5).reshape(2, local_rows, 3, heads_local, head_dim)

    if owners > WIDEST_SWITCH:
        slots = {"whole": rotate_by_bits(units, matching[0], owners)}
        return finish(project(reduce_by_halves, first_tokens, second_tokens, qkv_weight), slots, mine)

    helps = owners == 4 and groups == 2
    names = slot_units() if helps else {"whole": slot_units()["whole"]}

    def branch(move, busy, first_tokens, second_tokens, qkv_weight, units):
        slots = move(units)
        fresh = project(reduce_by_halves if busy else reduce_at_once, first_tokens, second_tokens, qkv_weight)
        filled = {
            name: slots[name] if name in slots else unwritten((count, *units.shape[1:]), units.dtype)
            for name, (_, count) in names.items()
        }
        return fresh, filled

    plans = [(functools.partial(move_alone, by=by, owners=owners), min(by, owners - by) > 1) for by in range(owners)]
    other, index = mine, jnp.clip(matching[0], 0, owners - 1)
    if helps:
        light_offsets = (0, 1, 3)
        plans += [
            (functools.partial(move_helped, heavy=heavy, by=by, owners=owners), by != 0)
            for heavy in range(2)
            for by in light_offsets
        ]
        other = lax.ppermute(mine, "grp", [(0, 1), (1, 0)])
        group, offset = lax.axis_index("grp"), index
        lends = sum((owners + 3 * group + i) << 4 * by for i, by in enumerate(light_offsets)) + (2 << 8)
        helped = (owners + 3 * (1 - group) + ((offset + 1) >> 1)) << 8
        alone = sum(offset << 4 * by for by in light_offsets)
        table = jnp.where(offset == 2, lends, alone + helped)
        index = (table >> (4 * other[0])) & 15
    branches = [functools.partial(branch, move, busy) for move, busy in plans]
    fresh, slots = lax.switch(index, branches, first_tokens, second_tokens, qkv_weight, units)
    return finish(fresh, slots, other)


def solution(mesh):
    in_specs = (
        P("grp", "tp"),
        P("grp", "tp"),
        P("tp", None, ("pp", "rep"), None),
        P(("grp", "tp"), None, None, ("pp", "rep"), None),
        P("grp"),
        P("grp"),
    )
    out_specs = (
        P(None, ("grp", "tp"), ("pp", "rep")),
        P(("grp", "tp"), None, None, ("pp", "rep"), None),
    )
    return jax.shard_map(shards, mesh=mesh, in_specs=in_specs, out_specs=out_specs, check_vma=False)
```

```python
import functools
import math

import jax
import jax.numpy as jnp
from jax import lax
from jax.experimental import pallas as pl
from jax.experimental.pallas import tpu as pltpu
from jax.sharding import PartitionSpec as P

WIDEST_SWITCH = 8


def shifted(block, axis, by):
    devices = lax.axis_size(axis)
    return lax.ppermute(block, axis, [(i, (i + by) % devices) for i in range(devices)])


def rotate_by_bits(block, offset, owners):
    for level in range((owners - 1).bit_length()):
        moved = shifted(block, "tp", 1 << level)
        block = jnp.where(offset >> level & 1 == 1, moved, block)
    return block


def reduce_by_halves(parts, owners):
    distances = list(range(owners))
    blocks = [parts[distance] for distance in distances]
    stride = 1
    while stride < owners:
        kept = [i for i, distance in enumerate(distances) if not distance & stride]
        gone = [i for i, distance in enumerate(distances) if distance & stride]
        sent = jnp.stack([blocks[i] for i in gone]).astype(jnp.bfloat16)
        got = lax.ppermute(sent, "tp", [(i, i ^ stride) for i in range(owners)]).astype(jnp.float32)
        blocks = [blocks[i] + got[j] for j, i in enumerate(kept)]
        distances = [distances[i] for i in kept]
        stride *= 2
    return blocks[0]


def reduce_at_once(parts, owners):
    total = parts[0]
    for distance in range(1, owners):
        pairs = [(i, i ^ distance) for i in range(owners)]
        total = total + lax.ppermute(parts[distance].astype(jnp.bfloat16), "tp", pairs).astype(jnp.float32)
    return total


UNITS = 8
LENT_TO_BUSY, LENT_TO_IDLE = 2, 3


def slot_units():
    return {
        "whole": (0, UNITS),
        "most": (0, UNITS - LENT_TO_BUSY),
        "own": (UNITS - LENT_TO_BUSY, LENT_TO_BUSY),
        "lent": (UNITS - LENT_TO_BUSY, LENT_TO_BUSY),
        "more": (0, UNITS - LENT_TO_IDLE),
        "lent_more": (UNITS - LENT_TO_IDLE, LENT_TO_IDLE),
    }


def slot_is_mine(name, mine, other):
    moves, lends, helps = mine != 0, (mine == 2) & (other != 2), (mine != 2) & (other == 2)
    return {
        "whole": moves & jnp.logical_not(lends | helps),
        "most": moves & (other != 0) & (lends | helps),
        "own": moves & helps,
        "lent": lends & (other != 0),
        "more": lends & (other == 0),
        "lent_more": lends & (other == 0),
    }[name]


def attention_kernel(names, lengths_ref, matching_ref, other_ref, total_ref, cache_ref, *refs):
    slots = dict(zip(names, refs))
    attended_ref, filled_ref, block, total, fresh, mixed, result, load_sems, row_sems, total_sem, result_sem = refs[len(names) :]
    part, _, heads, head_dim = block.shape[1:]
    steps, rows, kinds = fresh.shape[:3]
    reduced = pltpu.make_async_copy(total_ref, total, total_sem)
    reduced.start()
    per_row = UNITS // rows
    spots = per_row * part
    owners = lax.axis_size("tp")
    mine, other = matching_ref[0], other_ref[0]
    of_row = [block.at[pl.ds(r * per_row, per_row)] for r in range(rows)]
    arrivals = [pltpu.make_async_copy(cache_ref.at[pl.ds(r * per_row, per_row)], of_row[r], load_sems.at[r]) for r in range(rows)]
    stores = [pltpu.make_async_copy(of_row[r], filled_ref.at[pl.ds(r * per_row, per_row)], row_sems.at[r]) for r in range(rows)]

    def load(source, first, count):
        unit = first
        while unit < first + count:
            size = min(first + count, (unit // per_row + 1) * per_row) - unit
            pltpu.make_async_copy(
                source.at[pl.ds(unit - first, size)], block.at[pl.ds(unit, size)], load_sems.at[unit // per_row]
            ).start()
            unit += size

    @pl.when(mine == 0)
    def _():
        load(cache_ref, 0, UNITS)

    for name in names:

        @pl.when((mine != 0) if len(names) == 1 else slot_is_mine(name, mine, other))
        def _(name=name):
            load(slots[name], *slot_units()[name])

    first_row = lax.rem(lax.axis_index("tp") - matching_ref[0] + owners, owners) * rows
    first_head = lax.axis_index(("pp", "rep")) * heads
    level = heads.bit_length() - 1
    assert heads == 1 << level

    shape = (steps * heads, spots * heads)
    row, column = (lax.broadcasted_iota(jnp.int32, shape, axis) for axis in range(2))
    since = (row >> level) - (column >> level)
    allowed = jnp.where((row ^ column) & (heads - 1) == 0, since, -2 * spots)
    head = (first_head + 1 + (row & (heads - 1))).astype(jnp.float32)
    slope = jnp.exp(head * (-math.log(2.0) / 8.0))
    bias = slope * since.astype(jnp.float32)

    reduced.wait()
    for kind in range(kinds):
        for s in range(steps):
            for r in range(rows):
                for odd in range(2):
                    lanes = slice(odd * head_dim, (odd + 1) * head_dim)
                    fresh[s, r, kind, pl.ds(odd, heads // 2, 2), :] = total[kind, :, s * rows + r, lanes]
    for r in range(rows):
        at = lengths_ref[first_row + r]
        arrivals[r].wait()
        for s in range(steps):
            unit, spot = r * per_row + lax.div(at + s, part), lax.rem(at + s, part)
            for kind in range(2):
                block[unit, spot, kind] = fresh[s, r, 1 + kind].astype(block.dtype)
        stores[r].start()
    for r in range(rows):
        at = lengths_ref[first_row + r]
        query = fresh[:, r, 0].reshape(steps * heads, head_dim).astype(block.dtype)
        keys, values = (
            block[r * per_row : (r + 1) * per_row, :, kind].reshape(spots * heads, head_dim) for kind in range(2)
        )
        scores = lax.dot_general(query, keys, (((1,), (1,)), ((), ())), preferred_element_type=jnp.float32)
        scores = scores * head_dim ** (-0.5) - (bias + slope * at.astype(jnp.float32))
        scores = jnp.where(allowed + at >= 0, scores, -1e30)
        weights = jnp.exp(scores - jnp.max(scores, axis=1, keepdims=True)).astype(values.dtype)
        paired = jnp.concatenate([values, jnp.ones_like(values)], axis=1)
        mix = jnp.dot(weights, paired, preferred_element_type=jnp.float32)
        mixed[:, r] = (mix[:, :head_dim] / mix[:, head_dim:]).reshape(steps, heads, head_dim)
    for s in range(steps):
        for h in range(heads):
            result[s, :, h * head_dim : (h + 1) * head_dim] = mixed[s, :, h].astype(result.dtype)
    finish = pltpu.make_async_copy(result, attended_ref, result_sem)
    finish.start()
    for store in stores:
        store.wait()
    finish.wait()


def unwritten(shape, dtype):
    return pl.pallas_call(
        lambda out_ref: None,
        out_shape=jax.ShapeDtypeStruct(shape, dtype),
        out_specs=pl.BlockSpec(memory_space=pl.ANY),
        name="unwritten",
    )()


def attend_and_write(units, slots, total, rows, lengths, matching, other):
    heads, head_dim = units.shape[3:]
    kinds, steps = total.shape[0], total.shape[2] // rows
    smem = pl.BlockSpec(memory_space=pltpu.SMEM)
    anywhere = pl.BlockSpec(memory_space=pl.ANY)
    attended = jax.ShapeDtypeStruct((steps, rows, heads * head_dim), jnp.bfloat16)
    return pl.pallas_call(
        functools.partial(attention_kernel, tuple(slots)),
        out_shape=(attended, jax.ShapeDtypeStruct(units.shape, units.dtype)),
        in_specs=[smem, smem, smem, anywhere, anywhere] + [anywhere] * len(slots),
        out_specs=(anywhere, anywhere),
        scratch_shapes=[
            pltpu.VMEM(units.shape, units.dtype),
            pltpu.VMEM(total.shape, total.dtype),
            pltpu.VMEM((steps, rows, kinds, heads, head_dim), jnp.float32),
            pltpu.VMEM((steps, rows, heads, head_dim), jnp.float32),
            pltpu.VMEM(attended.shape, attended.dtype),
            pltpu.SemaphoreType.DMA((rows,)),
            pltpu.SemaphoreType.DMA((rows,)),
            pltpu.SemaphoreType.DMA,
            pltpu.SemaphoreType.DMA,
        ],
        compiler_params=pltpu.CompilerParams(vmem_limit_bytes=32 << 20),
        cost_estimate=pl.CostEstimate(flops=0, bytes_accessed=4 * units.size, transcendentals=0),
        name="attend",
    )(lengths, matching, other, total, units, *slots.values())


def projection_kernel(piece, first_ref, second_ref, weight_ref, parts_ref, sums):
    step = pl.program_id(0)
    kinds, pairs, _, width = sums.shape
    owners, rows = parts_ref.shape[0], parts_ref.shape[3]

    @pl.when(step == 0)
    def _():
        sums[...] = jnp.zeros_like(sums)

    count = owners * rows
    to, source = (lax.broadcasted_iota(jnp.int32, (count, count), axis) for axis in range(2))
    local_rows = rows // 2
    block, token_step, row = lax.div(to, rows), lax.div(lax.rem(to, rows), local_rows), lax.rem(to, local_rows)
    owner = block ^ lax.axis_index("tp")
    picks = (token_step * owners + owner) * local_rows + row == source
    picks = jnp.where(picks, 1.0, 0.0).astype(first_ref.dtype)
    pieces = weight_ref.shape[0] // piece

    def add(index, carry):
        kind = lax.rem(index, kinds)
        depth = pl.ds(pl.multiple_of(lax.div(index, kinds) * piece, piece), piece) if pieces > 1 else slice(None)
        tokens = jnp.concatenate([first_ref[:, depth], second_ref[:, depth]])
        tokens = jnp.dot(picks, tokens, preferred_element_type=jnp.float32).astype(tokens.dtype)
        by_head = jnp.swapaxes(weight_ref[depth, kind], 0, 1)
        for pair in range(pairs):
            both = jnp.concatenate([by_head[2 * pair], by_head[2 * pair + 1]], axis=1)
            sums[kind, pair] += jnp.dot(tokens, both, preferred_element_type=jnp.float32)
        return carry

    lax.fori_loop(0, pieces * kinds, add, 0)

    @pl.when(step == pl.num_programs(0) - 1)
    def _():
        for distance in range(owners):
            parts_ref[distance] = sums[:, :, distance * rows : (distance + 1) * rows]


def largest_divisor(number, most, unit):
    return max(size for size in range(unit, most + 1, unit) if number % size == 0)


def multiply(first_tokens, second_tokens, weight, owners):
    depth, kinds, heads, head_dim = weight.shape
    block = largest_divisor(depth, 512, 64)
    piece = 256 if block % 256 == 0 else block
    requests = first_tokens.shape[0]
    sums = (kinds, heads // 2, 2 * requests, 2 * head_dim)
    parts = (owners, kinds, heads // 2, 2 * requests // owners, 2 * head_dim)
    return pl.pallas_call(
        functools.partial(projection_kernel, piece),
        out_shape=jax.ShapeDtypeStruct(parts, jnp.float32),
        grid=(depth // block,),
        in_specs=[
            pl.BlockSpec((requests, block), lambda step: (0, step)),
            pl.BlockSpec((requests, block), lambda step: (0, step)),
            pl.BlockSpec((block, kinds, heads, head_dim), lambda step: (step, 0, 0, 0)),
        ],
        out_specs=pl.BlockSpec(parts, lambda step: (0,) * len(parts)),
        scratch_shapes=[pltpu.VMEM(sums, jnp.float32)],
        compiler_params=pltpu.CompilerParams(vmem_limit_bytes=48 << 20),
        cost_estimate=pl.CostEstimate(
            flops=4 * requests * weight.size, bytes_accessed=2 * weight.size, transcendentals=0
        ),
        name="project",
    )(first_tokens, second_tokens, weight)


def move_alone(units, by, owners):
    return {"whole": shifted(units, "tp", by)} if by else {}


def move_helped(units, heavy, by, owners):
    light = 1 - heavy

    def send(block, pairs):
        return lax.ppermute(block, ("grp", "tp"), pairs)

    def at(group, owner):
        return group * owners + owner % owners

    own = [(at(light, t), at(light, t + by)) for t in range(owners) if by]
    direct = [(at(heavy, t), at(heavy, t + 2)) for t in range(owners)] + own
    over = [(at(heavy, t), at(light, t)) for t in range(owners)]
    back = [(at(light, t), at(heavy, t + 2)) for t in range(owners)]
    split = UNITS - (LENT_TO_BUSY if by else LENT_TO_IDLE)
    most, last = units[:split], units[split:]
    lent = send(send(last, over), back)
    if by:
        return {"most": send(most, direct), "own": send(last, own), "lent": lent}
    return {"more": send(most, direct), "lent_more": lent}


def shards(first_tokens, second_tokens, qkv_weight, cache, lengths, matching):
    owners, groups = lax.axis_size("tp"), lax.axis_size("grp")
    assert owners & (owners - 1) == 0
    local_rows = cache.shape[0]
    units = cache.reshape(UNITS, -1, *cache.shape[2:])
    mine = matching[:1]

    def finish(total, slots, other):
        attended, filled = attend_and_write(units, slots, total, local_rows, lengths, matching, other)
        return attended, filled.reshape(cache.shape)

    def project(reduce, first_tokens, second_tokens, qkv_weight):
        return reduce(multiply(first_tokens, second_tokens, qkv_weight, owners), owners)

    if owners > WIDEST_SWITCH:
        slots = {"whole": rotate_by_bits(units, matching[0], owners)}
        return finish(project(reduce_by_halves, first_tokens, second_tokens, qkv_weight), slots, mine)

    helps = owners == 4 and groups == 2
    names = slot_units() if helps else {"whole": slot_units()["whole"]}

    def branch(move, busy, first_tokens, second_tokens, qkv_weight, units):
        slots = move(units)
        total = project(reduce_by_halves if busy else reduce_at_once, first_tokens, second_tokens, qkv_weight)
        filled = {
            name: slots[name] if name in slots else unwritten((count, *units.shape[1:]), units.dtype)
            for name, (_, count) in names.items()
        }
        return total, filled

    plans = [(functools.partial(move_alone, by=by, owners=owners), min(by, owners - by) > 1) for by in range(owners)]
    other, index = mine, jnp.clip(matching[0], 0, owners - 1)
    if helps:
        light_offsets = (0, 1, 3)
        plans += [
            (functools.partial(move_helped, heavy=heavy, by=by, owners=owners), by != 0)
            for heavy in range(2)
            for by in light_offsets
        ]
        other = lax.ppermute(mine, "grp", [(0, 1), (1, 0)])
        group, offset = lax.axis_index("grp"), index
        lends = sum((owners + 3 * group + i) << 4 * by for i, by in enumerate(light_offsets)) + (2 << 8)
        helped = (owners + 3 * (1 - group) + ((offset + 1) >> 1)) << 8
        alone = sum(offset << 4 * by for by in light_offsets)
        table = jnp.where(offset == 2, lends, alone + helped)
        index = (table >> (4 * other[0])) & 15
    branches = [functools.partial(branch, move, busy) for move, busy in plans]
    total, slots = lax.switch(index, branches, first_tokens, second_tokens, qkv_weight, units)
    return finish(total, slots, other)


def solution(mesh):
    in_specs = (
        P("grp", "tp"),
        P("grp", "tp"),
        P("tp", None, ("pp", "rep"), None),
        P(("grp", "tp"), None, None, ("pp", "rep"), None),
        P("grp"),
        P("grp"),
    )
    out_specs = (
        P(None, ("grp", "tp"), ("pp", "rep")),
        P(("grp", "tp"), None, None, ("pp", "rep"), None),
    )
    return jax.shard_map(shards, mesh=mesh, in_specs=in_specs, out_specs=out_specs, check_vma=False)
```

```python
import functools
import math

import jax
import jax.numpy as jnp
from jax import lax
from jax.experimental import pallas as pl
from jax.experimental.pallas import tpu as pltpu
from jax.sharding import PartitionSpec as P

WIDEST_SWITCH = 8


def shifted(block, axis, by):
    devices = lax.axis_size(axis)
    return lax.ppermute(block, axis, [(i, (i + by) % devices) for i in range(devices)])


def rotate_by_bits(block, offset, owners):
    for level in range((owners - 1).bit_length()):
        moved = shifted(block, "tp", 1 << level)
        block = jnp.where(offset >> level & 1 == 1, moved, block)
    return block


def reduce_by_halves(parts, owners):
    distances = list(range(owners))
    blocks = [parts[distance] for distance in distances]
    stride = 1
    while stride < owners:
        kept = [i for i, distance in enumerate(distances) if not distance & stride]
        gone = [i for i, distance in enumerate(distances) if distance & stride]
        sent = jnp.stack([blocks[i] for i in gone]).astype(jnp.bfloat16)
        got = lax.ppermute(sent, "tp", [(i, i ^ stride) for i in range(owners)]).astype(jnp.float32)
        blocks = [blocks[i] + got[j] for j, i in enumerate(kept)]
        distances = [distances[i] for i in kept]
        stride *= 2
    return blocks[0]


def reduce_at_once(parts, owners):
    total = parts[0]
    for distance in range(1, owners):
        pairs = [(i, i ^ distance) for i in range(owners)]
        total = total + lax.ppermute(parts[distance].astype(jnp.bfloat16), "tp", pairs).astype(jnp.float32)
    return total


UNITS = 8
LENT_TO_BUSY, LENT_TO_IDLE = 2, 3


def slot_units():
    return {
        "whole": (0, UNITS),
        "most": (0, UNITS - LENT_TO_BUSY),
        "own": (UNITS - LENT_TO_BUSY, LENT_TO_BUSY),
        "lent": (UNITS - LENT_TO_BUSY, LENT_TO_BUSY),
        "more": (0, UNITS - LENT_TO_IDLE),
        "lent_more": (UNITS - LENT_TO_IDLE, LENT_TO_IDLE),
    }


def slot_is_mine(name, mine, other):
    moves, helps = mine != 0, (mine != 2) & (other == 2)
    lends = jnp.where(other == 0, moves, (mine == 2) & (other != 2))
    return {
        "whole": moves & jnp.logical_not(lends | helps),
        "most": moves & (other != 0) & (lends | helps),
        "own": moves & helps,
        "lent": lends & (other != 0),
        "more": lends & (other == 0),
        "lent_more": lends & (other == 0),
    }[name]


def attention_kernel(names, lengths_ref, matching_ref, other_ref, total_ref, cache_ref, *refs):
    slots = dict(zip(names, refs))
    attended_ref, filled_ref, block, total, fresh, mixed, result, load_sems, row_sems, total_sem, result_sem = refs[len(names) :]
    part, _, heads, head_dim = block.shape[1:]
    steps, rows, kinds = fresh.shape[:3]
    reduced = pltpu.make_async_copy(total_ref, total, total_sem)
    reduced.start()
    per_row = UNITS // rows
    spots = per_row * part
    owners = lax.axis_size("tp")
    mine, other = matching_ref[0], other_ref[0]
    of_row = [block.at[pl.ds(r * per_row, per_row)] for r in range(rows)]
    arrivals = [pltpu.make_async_copy(cache_ref.at[pl.ds(r * per_row, per_row)], of_row[r], load_sems.at[r]) for r in range(rows)]
    stores = [pltpu.make_async_copy(of_row[r], filled_ref.at[pl.ds(r * per_row, per_row)], row_sems.at[r]) for r in range(rows)]

    def load(source, first, count):
        unit = first
        while unit < first + count:
            size = min(first + count, (unit // per_row + 1) * per_row) - unit
            pltpu.make_async_copy(
                source.at[pl.ds(unit - first, size)], block.at[pl.ds(unit, size)], load_sems.at[unit // per_row]
            ).start()
            unit += size

    @pl.when(mine == 0)
    def _():
        load(cache_ref, 0, UNITS)

    for name in names:

        @pl.when((mine != 0) if len(names) == 1 else slot_is_mine(name, mine, other))
        def _(name=name):
            load(slots[name], *slot_units()[name])

    first_row = lax.rem(lax.axis_index("tp") - matching_ref[0] + owners, owners) * rows
    first_head = lax.axis_index(("pp", "rep")) * heads
    level = heads.bit_length() - 1
    assert heads == 1 << level

    shape = (steps * heads, spots * heads)
    row, column = (lax.broadcasted_iota(jnp.int32, shape, axis) for axis in range(2))
    since = (row >> level) - (column >> level)
    allowed = jnp.where((row ^ column) & (heads - 1) == 0, since, -2 * spots)
    head = (first_head + 1 + (row & (heads - 1))).astype(jnp.float32)
    slope = jnp.exp(head * (-math.log(2.0) / 8.0))
    bias = slope * since.astype(jnp.float32)

    reduced.wait()
    for kind in range(kinds):
        for s in range(steps):
            for r in range(rows):
                for odd in range(2):
                    lanes = slice(odd * head_dim, (odd + 1) * head_dim)
                    fresh[s, r, kind, pl.ds(odd, heads // 2, 2), :] = total[kind, :, s * rows + r, lanes]
    for r in range(rows):
        at = lengths_ref[first_row + r]
        arrivals[r].wait()
        for s in range(steps):
            unit, spot = r * per_row + lax.div(at + s, part), lax.rem(at + s, part)
            for kind in range(2):
                block[unit, spot, kind] = fresh[s, r, 1 + kind].astype(block.dtype)
        stores[r].start()
    for r in range(rows):
        at = lengths_ref[first_row + r]
        query = fresh[:, r, 0].reshape(steps * heads, head_dim).astype(block.dtype)
        keys, values = (
            block[r * per_row : (r + 1) * per_row, :, kind].reshape(spots * heads, head_dim) for kind in range(2)
        )
        scores = lax.dot_general(query, keys, (((1,), (1,)), ((), ())), preferred_element_type=jnp.float32)
        scores = scores * head_dim ** (-0.5) - (bias + slope * at.astype(jnp.float32))
        scores = jnp.where(allowed + at >= 0, scores, -1e30)
        weights = jnp.exp(scores - jnp.max(scores, axis=1, keepdims=True)).astype(values.dtype)
        paired = jnp.concatenate([values, jnp.ones_like(values)], axis=1)
        mix = jnp.dot(weights, paired, preferred_element_type=jnp.float32)
        mixed[:, r] = (mix[:, :head_dim] / mix[:, head_dim:]).reshape(steps, heads, head_dim)
    for s in range(steps):
        for h in range(heads):
            result[s, :, h * head_dim : (h + 1) * head_dim] = mixed[s, :, h].astype(result.dtype)
    finish = pltpu.make_async_copy(result, attended_ref, result_sem)
    finish.start()
    for store in stores:
        store.wait()
    finish.wait()


def unwritten(shape, dtype):
    return pl.pallas_call(
        lambda out_ref: None,
        out_shape=jax.ShapeDtypeStruct(shape, dtype),
        out_specs=pl.BlockSpec(memory_space=pl.ANY),
        name="unwritten",
    )()


def attend_and_write(units, slots, total, rows, lengths, matching, other):
    heads, head_dim = units.shape[3:]
    kinds, steps = total.shape[0], total.shape[2] // rows
    smem = pl.BlockSpec(memory_space=pltpu.SMEM)
    anywhere = pl.BlockSpec(memory_space=pl.ANY)
    attended = jax.ShapeDtypeStruct((steps, rows, heads * head_dim), jnp.bfloat16)
    return pl.pallas_call(
        functools.partial(attention_kernel, tuple(slots)),
        out_shape=(attended, jax.ShapeDtypeStruct(units.shape, units.dtype)),
        in_specs=[smem, smem, smem, anywhere, anywhere] + [anywhere] * len(slots),
        out_specs=(anywhere, anywhere),
        scratch_shapes=[
            pltpu.VMEM(units.shape, units.dtype),
            pltpu.VMEM(total.shape, total.dtype),
            pltpu.VMEM((steps, rows, kinds, heads, head_dim), jnp.float32),
            pltpu.VMEM((steps, rows, heads, head_dim), jnp.float32),
            pltpu.VMEM(attended.shape, attended.dtype),
            pltpu.SemaphoreType.DMA((rows,)),
            pltpu.SemaphoreType.DMA((rows,)),
            pltpu.SemaphoreType.DMA,
            pltpu.SemaphoreType.DMA,
        ],
        compiler_params=pltpu.CompilerParams(vmem_limit_bytes=32 << 20),
        cost_estimate=pl.CostEstimate(flops=0, bytes_accessed=4 * units.size, transcendentals=0),
        name="attend",
    )(lengths, matching, other, total, units, *slots.values())


def projection_kernel(piece, first_ref, second_ref, weight_ref, parts_ref, sums):
    step = pl.program_id(0)
    kinds, pairs, _, width = sums.shape
    owners, rows = parts_ref.shape[0], parts_ref.shape[3]

    @pl.when(step == 0)
    def _():
        sums[...] = jnp.zeros_like(sums)

    count = owners * rows
    to, source = (lax.broadcasted_iota(jnp.int32, (count, count), axis) for axis in range(2))
    local_rows = rows // 2
    block, token_step, row = lax.div(to, rows), lax.div(lax.rem(to, rows), local_rows), lax.rem(to, local_rows)
    owner = block ^ lax.axis_index("tp")
    picks = (token_step * owners + owner) * local_rows + row == source
    picks = jnp.where(picks, 1.0, 0.0).astype(first_ref.dtype)
    pieces = weight_ref.shape[0] // piece

    def add(index, carry):
        kind = lax.rem(index, kinds)
        depth = pl.ds(pl.multiple_of(lax.div(index, kinds) * piece, piece), piece) if pieces > 1 else slice(None)
        tokens = jnp.concatenate([first_ref[:, depth], second_ref[:, depth]])
        tokens = jnp.dot(picks, tokens, preferred_element_type=jnp.float32).astype(tokens.dtype)
        by_head = jnp.swapaxes(weight_ref[depth, kind], 0, 1)
        for pair in range(pairs):
            both = jnp.concatenate([by_head[2 * pair], by_head[2 * pair + 1]], axis=1)
            sums[kind, pair] += jnp.dot(tokens, both, preferred_element_type=jnp.float32)
        return carry

    lax.fori_loop(0, pieces * kinds, add, 0)

    @pl.when(step == pl.num_programs(0) - 1)
    def _():
        for distance in range(owners):
            parts_ref[distance] = sums[:, :, distance * rows : (distance + 1) * rows]


def largest_divisor(number, most, unit):
    return max(size for size in range(unit, most + 1, unit) if number % size == 0)


def multiply(first_tokens, second_tokens, weight, owners, start=0.0, end=1.0):
    depth, kinds, heads, head_dim = weight.shape
    block = largest_divisor(depth, 512, 64)
    piece = 256 if block % 256 == 0 else block
    requests = first_tokens.shape[0]
    sums = (kinds, heads // 2, 2 * requests, 2 * head_dim)
    parts = (owners, kinds, heads // 2, 2 * requests // owners, 2 * head_dim)
    begin, until = (int(depth // block * at) for at in (start, end))
    return pl.pallas_call(
        functools.partial(projection_kernel, piece),
        out_shape=jax.ShapeDtypeStruct(parts, jnp.float32),
        grid=(until - begin,),
        in_specs=[
            pl.BlockSpec((requests, block), lambda step: (0, begin + step)),
            pl.BlockSpec((requests, block), lambda step: (0, begin + step)),
            pl.BlockSpec((block, kinds, heads, head_dim), lambda step: (begin + step, 0, 0, 0)),
        ],
        out_specs=pl.BlockSpec(parts, lambda step: (0,) * len(parts)),
        scratch_shapes=[pltpu.VMEM(sums, jnp.float32)],
        compiler_params=pltpu.CompilerParams(vmem_limit_bytes=48 << 20),
        cost_estimate=pl.CostEstimate(
            flops=4 * requests * weight.size, bytes_accessed=2 * weight.size, transcendentals=0
        ),
        name="project",
    )(first_tokens, second_tokens, weight)


def move_alone(units, by, owners):
    return ({"whole": shifted(units, "tp", by)} if by else {}), None


def move_helped(units, heavy, far, by, owners):
    light = 1 - heavy

    def send(block, pairs):
        return lax.ppermute(block, ("grp", "tp"), pairs)

    def at(group, owner):
        return group * owners + owner % owners

    own = [(at(light, t), at(light, t + by)) for t in range(owners) if by]
    direct = [(at(heavy, t), at(heavy, t + far)) for t in range(owners)] + own
    over = [(at(heavy, t), at(light, t)) for t in range(owners)]
    back = [(at(light, t), at(heavy, t + far)) for t in range(owners)]
    split = UNITS - (LENT_TO_BUSY if by else LENT_TO_IDLE)
    most, last = units[:split], units[split:]
    lent_over = send(last, over)
    lent = send(lent_over, back)
    if by:
        return {"most": send(most, direct), "own": send(last, own), "lent": lent}, None
    return {"more": send(most, direct), "lent_more": lent}, lent_over if far != 2 else None


def shards(first_tokens, second_tokens, qkv_weight, cache, lengths, matching):
    owners, groups = lax.axis_size("tp"), lax.axis_size("grp")
    assert owners & (owners - 1) == 0
    local_rows = cache.shape[0]
    units = cache.reshape(UNITS, -1, *cache.shape[2:])
    mine = matching[:1]

    def finish(total, slots, other):
        attended, filled = attend_and_write(units, slots, total, local_rows, lengths, matching, other)
        return attended, filled.reshape(cache.shape)

    def project(reduce, behind, first_tokens, second_tokens, qkv_weight):
        if behind is None:
            return reduce(multiply(first_tokens, second_tokens, qkv_weight, owners), owners)
        parts = multiply(first_tokens, second_tokens, qkv_weight, owners, 0.0, 0.5)
        first_tokens, _ = lax.optimization_barrier((first_tokens, behind))
        return reduce(parts + multiply(first_tokens, second_tokens, qkv_weight, owners, 0.5, 1.0), owners)

    if owners > WIDEST_SWITCH:
        slots = {"whole": rotate_by_bits(units, matching[0], owners)}
        return finish(project(reduce_by_halves, None, first_tokens, second_tokens, qkv_weight), slots, mine)

    helps = owners == 4 and groups == 2
    names = slot_units() if helps else {"whole": slot_units()["whole"]}

    def branch(move, busy, first_tokens, second_tokens, qkv_weight, units):
        slots, behind = move(units)
        total = project(reduce_by_halves if busy else reduce_at_once, behind, first_tokens, second_tokens, qkv_weight)
        filled = {
            name: slots[name] if name in slots else unwritten((count, *units.shape[1:]), units.dtype)
            for name, (_, count) in names.items()
        }
        return total, filled

    plans = [(functools.partial(move_alone, by=by, owners=owners), min(by, owners - by) > 1) for by in range(owners)]
    other, index = mine, jnp.clip(matching[0], 0, owners - 1)
    if helps:
        helped = [(2, 0), (2, 1), (2, 3), (1, 0), (3, 0)]
        plans += [
            (functools.partial(move_helped, heavy=heavy, far=far, by=by, owners=owners), by != 0)
            for heavy in range(2)
            for far, by in helped
        ]
        other = lax.ppermute(mine, "grp", [(0, 1), (1, 0)])
        group, offset = lax.axis_index("grp"), index
        first, second = owners + len(helped) * group, owners + len(helped) * (1 - group)
        table = 0
        for its in range(owners):
            entry = offset
            for i, (far, by) in enumerate(helped):
                if by == its:
                    entry = jnp.where(offset == far, first + i, entry)
                if far == its:
                    entry = jnp.where(offset == by, second + i, entry)
            table = table + (entry << 4 * its)
        index = (table >> (4 * other[0])) & 15
    branches = [functools.partial(branch, move, busy) for move, busy in plans]
    total, slots = lax.switch(index, branches, first_tokens, second_tokens, qkv_weight, units)
    return finish(total, slots, other)


def solution(mesh):
    in_specs = (
        P("grp", "tp"),
        P("grp", "tp"),
        P("tp", None, ("pp", "rep"), None),
        P(("grp", "tp"), None, None, ("pp", "rep"), None),
        P("grp"),
        P("grp"),
    )
    out_specs = (
        P(None, ("grp", "tp"), ("pp", "rep")),
        P(("grp", "tp"), None, None, ("pp", "rep"), None),
    )
    return jax.shard_map(shards, mesh=mesh, in_specs=in_specs, out_specs=out_specs, check_vma=False)
```

```python
import functools
import math

import jax
import jax.numpy as jnp
from jax import lax
from jax.experimental import pallas as pl
from jax.experimental.pallas import tpu as pltpu
from jax.sharding import PartitionSpec as P

WIDEST_SWITCH = 8


def shifted(block, axis, by):
    devices = lax.axis_size(axis)
    return lax.ppermute(block, axis, [(i, (i + by) % devices) for i in range(devices)])


def rotate_by_bits(block, offset, owners):
    for level in range((owners - 1).bit_length()):
        moved = shifted(block, "tp", 1 << level)
        block = jnp.where(offset >> level & 1 == 1, moved, block)
    return block


def reduce_by_halves(parts, owners):
    distances = list(range(owners))
    blocks = [parts[distance] for distance in distances]
    stride = 1
    while stride < owners:
        kept = [i for i, distance in enumerate(distances) if not distance & stride]
        gone = [i for i, distance in enumerate(distances) if distance & stride]
        sent = jnp.stack([blocks[i] for i in gone]).astype(jnp.bfloat16)
        got = lax.ppermute(sent, "tp", [(i, i ^ stride) for i in range(owners)]).astype(jnp.float32)
        blocks = [blocks[i] + got[j] for j, i in enumerate(kept)]
        distances = [distances[i] for i in kept]
        stride *= 2
    return blocks[0]


def reduce_at_once(parts, owners):
    total = parts[0]
    for distance in reversed(range(1, owners)):
        pairs = [(i, i ^ distance) for i in range(owners)]
        total = total + lax.ppermute(parts[distance].astype(jnp.bfloat16), "tp", pairs).astype(jnp.float32)
    return total


UNITS = 8
LENT_TO_BUSY, LENT_TO_IDLE = 2, 3


def slot_units():
    return {
        "whole": (0, UNITS),
        "most": (0, UNITS - LENT_TO_BUSY),
        "own": (UNITS - LENT_TO_BUSY, LENT_TO_BUSY),
        "lent": (UNITS - LENT_TO_BUSY, LENT_TO_BUSY),
        "more": (0, UNITS - LENT_TO_IDLE),
        "lent_more": (UNITS - LENT_TO_IDLE, LENT_TO_IDLE),
    }


def slot_is_mine(name, mine, other):
    moves, helps = mine != 0, (mine != 2) & (other == 2)
    lends = jnp.where(other == 0, moves, (mine == 2) & (other != 2))
    return {
        "whole": moves & jnp.logical_not(lends | helps),
        "most": moves & (other != 0) & (lends | helps),
        "own": moves & helps,
        "lent": lends & (other != 0),
        "more": lends & (other == 0),
        "lent_more": lends & (other == 0),
    }[name]


def attention_kernel(names, lengths_ref, matching_ref, other_ref, total_ref, cache_ref, *refs):
    slots = dict(zip(names, refs))
    attended_ref, filled_ref, block, total, fresh, mixed, result, load_sems, row_sems, total_sem, result_sem = refs[len(names) :]
    part, _, heads, head_dim = block.shape[1:]
    steps, rows, kinds = fresh.shape[:3]
    reduced = pltpu.make_async_copy(total_ref, total, total_sem)
    reduced.start()
    per_row = UNITS // rows
    spots = per_row * part
    owners = lax.axis_size("tp")
    mine, other = matching_ref[0], other_ref[0]
    of_row = [block.at[pl.ds(r * per_row, per_row)] for r in range(rows)]
    arrivals = [pltpu.make_async_copy(cache_ref.at[pl.ds(r * per_row, per_row)], of_row[r], load_sems.at[r]) for r in range(rows)]
    stores = [pltpu.make_async_copy(of_row[r], filled_ref.at[pl.ds(r * per_row, per_row)], row_sems.at[r]) for r in range(rows)]

    def load(source, first, count):
        unit = first
        while unit < first + count:
            size = min(first + count, (unit // per_row + 1) * per_row) - unit
            pltpu.make_async_copy(
                source.at[pl.ds(unit - first, size)], block.at[pl.ds(unit, size)], load_sems.at[unit // per_row]
            ).start()
            unit += size

    @pl.when(mine == 0)
    def _():
        load(cache_ref, 0, UNITS)

    for name in names:

        @pl.when((mine != 0) if len(names) == 1 else slot_is_mine(name, mine, other))
        def _(name=name):
            load(slots[name], *slot_units()[name])

    first_row = lax.rem(lax.axis_index("tp") - matching_ref[0] + owners, owners) * rows
    first_head = lax.axis_index(("pp", "rep")) * heads
    level = heads.bit_length() - 1
    assert heads == 1 << level

    shape = (steps * heads, spots * heads)
    row, column = (lax.broadcasted_iota(jnp.int32, shape, axis) for axis in range(2))
    since = (row >> level) - (column >> level)
    allowed = jnp.where((row ^ column) & (heads - 1) == 0, since, -2 * spots)
    head = (first_head + 1 + (row & (heads - 1))).astype(jnp.float32)
    slope = jnp.exp(head * (-math.log(2.0) / 8.0))
    bias = slope * since.astype(jnp.float32)

    reduced.wait()
    for kind in range(kinds):
        for s in range(steps):
            for r in range(rows):
                for odd in range(2):
                    lanes = slice(odd * head_dim, (odd + 1) * head_dim)
                    fresh[s, r, kind, pl.ds(odd, heads // 2, 2), :] = total[kind, :, s * rows + r, lanes]
    for r in range(rows):
        at = lengths_ref[first_row + r]
        arrivals[r].wait()
        for s in range(steps):
            unit, spot = r * per_row + lax.div(at + s, part), lax.rem(at + s, part)
            for kind in range(2):
                block[unit, spot, kind] = fresh[s, r, 1 + kind].astype(block.dtype)
        stores[r].start()
    for r in range(rows):
        at = lengths_ref[first_row + r]
        query = fresh[:, r, 0].reshape(steps * heads, head_dim).astype(block.dtype)
        keys, values = (
            block[r * per_row : (r + 1) * per_row, :, kind].reshape(spots * heads, head_dim) for kind in range(2)
        )
        scores = lax.dot_general(query, keys, (((1,), (1,)), ((), ())), preferred_element_type=jnp.float32)
        scores = scores * head_dim ** (-0.5) - (bias + slope * at.astype(jnp.float32))
        scores = jnp.where(allowed + at >= 0, scores, -1e30)
        weights = jnp.exp(scores - jnp.max(scores, axis=1, keepdims=True)).astype(values.dtype)
        paired = jnp.concatenate([values, jnp.ones_like(values)], axis=1)
        mix = jnp.dot(weights, paired, preferred_element_type=jnp.float32)
        mixed[:, r] = (mix[:, :head_dim] / mix[:, head_dim:]).reshape(steps, heads, head_dim)
    for s in range(steps):
        for h in range(heads):
            result[s, :, h * head_dim : (h + 1) * head_dim] = mixed[s, :, h].astype(result.dtype)
    finish = pltpu.make_async_copy(result, attended_ref, result_sem)
    finish.start()
    for store in stores:
        store.wait()
    finish.wait()


def unwritten(shape, dtype):
    return pl.pallas_call(
        lambda out_ref: None,
        out_shape=jax.ShapeDtypeStruct(shape, dtype),
        out_specs=pl.BlockSpec(memory_space=pl.ANY),
        name="unwritten",
    )()


def attend_and_write(units, slots, total, rows, lengths, matching, other):
    heads, head_dim = units.shape[3:]
    kinds, steps = total.shape[0], total.shape[2] // rows
    smem = pl.BlockSpec(memory_space=pltpu.SMEM)
    anywhere = pl.BlockSpec(memory_space=pl.ANY)
    attended = jax.ShapeDtypeStruct((steps, rows, heads * head_dim), jnp.bfloat16)
    return pl.pallas_call(
        functools.partial(attention_kernel, tuple(slots)),
        out_shape=(attended, jax.ShapeDtypeStruct(units.shape, units.dtype)),
        in_specs=[smem, smem, smem, anywhere, anywhere] + [anywhere] * len(slots),
        out_specs=(anywhere, anywhere),
        scratch_shapes=[
            pltpu.VMEM(units.shape, units.dtype),
            pltpu.VMEM(total.shape, total.dtype),
            pltpu.VMEM((steps, rows, kinds, heads, head_dim), jnp.float32),
            pltpu.VMEM((steps, rows, heads, head_dim), jnp.float32),
            pltpu.VMEM(attended.shape, attended.dtype),
            pltpu.SemaphoreType.DMA((rows,)),
            pltpu.SemaphoreType.DMA((rows,)),
            pltpu.SemaphoreType.DMA,
            pltpu.SemaphoreType.DMA,
        ],
        compiler_params=pltpu.CompilerParams(vmem_limit_bytes=32 << 20),
        cost_estimate=pl.CostEstimate(flops=0, bytes_accessed=4 * units.size, transcendentals=0),
        name="attend",
    )(lengths, matching, other, total, units, *slots.values())


def projection_kernel(piece, first_ref, second_ref, weight_ref, parts_ref, sums):
    step = pl.program_id(0)
    kinds, pairs, _, width = sums.shape
    owners, rows = parts_ref.shape[0], parts_ref.shape[3]

    @pl.when(step == 0)
    def _():
        sums[...] = jnp.zeros_like(sums)

    count = owners * rows
    to, source = (lax.broadcasted_iota(jnp.int32, (count, count), axis) for axis in range(2))
    local_rows = rows // 2
    block, token_step, row = lax.div(to, rows), lax.div(lax.rem(to, rows), local_rows), lax.rem(to, local_rows)
    owner = block ^ lax.axis_index("tp")
    picks = (token_step * owners + owner) * local_rows + row == source
    picks = jnp.where(picks, 1.0, 0.0).astype(first_ref.dtype)
    pieces = weight_ref.shape[0] // piece

    def add(index, carry):
        kind = lax.rem(index, kinds)
        depth = pl.ds(pl.multiple_of(lax.div(index, kinds) * piece, piece), piece) if pieces > 1 else slice(None)
        tokens = jnp.concatenate([first_ref[:, depth], second_ref[:, depth]])
        tokens = jnp.dot(picks, tokens, preferred_element_type=jnp.float32).astype(tokens.dtype)
        by_head = jnp.swapaxes(weight_ref[depth, kind], 0, 1)
        for pair in range(pairs):
            both = jnp.concatenate([by_head[2 * pair], by_head[2 * pair + 1]], axis=1)
            sums[kind, pair] += jnp.dot(tokens, both, preferred_element_type=jnp.float32)
        return carry

    lax.fori_loop(0, pieces * kinds, add, 0)

    @pl.when(step == pl.num_programs(0) - 1)
    def _():
        for distance in range(owners):
            parts_ref[distance] = sums[:, :, distance * rows : (distance + 1) * rows]


def largest_divisor(number, most, unit):
    return max(size for size in range(unit, most + 1, unit) if number % size == 0)


def multiply(first_tokens, second_tokens, weight, owners, start=0.0, end=1.0):
    depth, kinds, heads, head_dim = weight.shape
    block = largest_divisor(depth, 512, 64)
    piece = 256 if block % 256 == 0 else block
    requests = first_tokens.shape[0]
    sums = (kinds, heads // 2, 2 * requests, 2 * head_dim)
    parts = (owners, kinds, heads // 2, 2 * requests // owners, 2 * head_dim)
    begin, until = (int(depth // block * at) for at in (start, end))
    return pl.pallas_call(
        functools.partial(projection_kernel, piece),
        out_shape=jax.ShapeDtypeStruct(parts, jnp.float32),
        grid=(until - begin,),
        in_specs=[
            pl.BlockSpec((requests, block), lambda step: (0, begin + step)),
            pl.BlockSpec((requests, block), lambda step: (0, begin + step)),
            pl.BlockSpec((block, kinds, heads, head_dim), lambda step: (begin + step, 0, 0, 0)),
        ],
        out_specs=pl.BlockSpec(parts, lambda step: (0,) * len(parts)),
        scratch_shapes=[pltpu.VMEM(sums, jnp.float32)],
        compiler_params=pltpu.CompilerParams(vmem_limit_bytes=48 << 20),
        cost_estimate=pl.CostEstimate(
            flops=4 * requests * weight.size, bytes_accessed=2 * weight.size, transcendentals=0
        ),
        name="project",
    )(first_tokens, second_tokens, weight)


def move_alone(units, by, owners):
    return ({"whole": shifted(units, "tp", by)} if by else {}), None


def move_helped(units, heavy, far, by, owners):
    light = 1 - heavy

    def send(block, pairs):
        return lax.ppermute(block, ("grp", "tp"), pairs)

    def at(group, owner):
        return group * owners + owner % owners

    own = [(at(light, t), at(light, t + by)) for t in range(owners) if by]
    direct = [(at(heavy, t), at(heavy, t + far)) for t in range(owners)] + own
    over = [(at(heavy, t), at(light, t)) for t in range(owners)]
    back = [(at(light, t), at(heavy, t + far)) for t in range(owners)]
    split = UNITS - (LENT_TO_BUSY if by else LENT_TO_IDLE)
    most, last = units[:split], units[split:]
    lent_over = send(last, over)
    lent = send(lent_over, back)
    if by:
        return {"most": send(most, direct), "own": send(last, own), "lent": lent}, None
    return {"more": send(most, direct), "lent_more": lent}, lent_over if far != 2 else None


def shards(first_tokens, second_tokens, qkv_weight, cache, lengths, matching):
    owners, groups = lax.axis_size("tp"), lax.axis_size("grp")
    assert owners & (owners - 1) == 0
    local_rows = cache.shape[0]
    units = cache.reshape(UNITS, -1, *cache.shape[2:])
    mine = matching[:1]

    def finish(total, slots, other):
        attended, filled = attend_and_write(units, slots, total, local_rows, lengths, matching, other)
        return attended, filled.reshape(cache.shape)

    def project(reduce, behind, first_tokens, second_tokens, qkv_weight):
        if behind is None:
            return reduce(multiply(first_tokens, second_tokens, qkv_weight, owners), owners)
        parts = multiply(first_tokens, second_tokens, qkv_weight, owners, 0.0, 0.5)
        first_tokens, _ = lax.optimization_barrier((first_tokens, behind))
        return reduce(parts + multiply(first_tokens, second_tokens, qkv_weight, owners, 0.5, 1.0), owners)

    if owners > WIDEST_SWITCH:
        slots = {"whole": rotate_by_bits(units, matching[0], owners)}
        return finish(project(reduce_by_halves, None, first_tokens, second_tokens, qkv_weight), slots, mine)

    helps = owners == 4 and groups == 2
    names = slot_units() if helps else {"whole": slot_units()["whole"]}

    def branch(move, busy, first_tokens, second_tokens, qkv_weight, units):
        slots, behind = move(units)
        total = project(reduce_by_halves if busy else reduce_at_once, behind, first_tokens, second_tokens, qkv_weight)
        filled = {
            name: slots[name] if name in slots else unwritten((count, *units.shape[1:]), units.dtype)
            for name, (_, count) in names.items()
        }
        return total, filled

    plans = [(functools.partial(move_alone, by=by, owners=owners), min(by, owners - by) > 1) for by in range(owners)]
    other, index = mine, jnp.clip(matching[0], 0, owners - 1)
    if helps:
        helped = [(2, 0), (2, 1), (2, 3), (1, 0), (3, 0)]
        plans += [
            (functools.partial(move_helped, heavy=heavy, far=far, by=by, owners=owners), by != 0)
            for heavy in range(2)
            for far, by in helped
        ]
        other = lax.ppermute(mine, "grp", [(0, 1), (1, 0)])
        group, offset = lax.axis_index("grp"), index
        first, second = owners + len(helped) * group, owners + len(helped) * (1 - group)
        table = 0
        for its in range(owners):
            entry = offset
            for i, (far, by) in enumerate(helped):
                if by == its:
                    entry = jnp.where(offset == far, first + i, entry)
                if far == its:
                    entry = jnp.where(offset == by, second + i, entry)
            table = table + (entry << 4 * its)
        index = (table >> (4 * other[0])) & 15
    branches = [functools.partial(branch, move, busy) for move, busy in plans]
    total, slots = lax.switch(index, branches, first_tokens, second_tokens, qkv_weight, units)
    return finish(total, slots, other)


def solution(mesh):
    in_specs = (
        P("grp", "tp"),
        P("grp", "tp"),
        P("tp", None, ("pp", "rep"), None),
        P(("grp", "tp"), None, None, ("pp", "rep"), None),
        P("grp"),
        P("grp"),
    )
    out_specs = (
        P(None, ("grp", "tp"), ("pp", "rep")),
        P(("grp", "tp"), None, None, ("pp", "rep"), None),
    )
    return jax.shard_map(shards, mesh=mesh, in_specs=in_specs, out_specs=out_specs, check_vma=False)
```
